32 devices in a mesh: gx: 4 (over z), gy: 8 (over y, x, core).
Axes of the slice: x: 2, y: 2, z: 4, core: 2. Of those that a mesh axis runs over, the one named last changes fastest.
Arguments:
- source_term: float32 [512, 125], P(('gx', 'gy')), may hold values from -24 to 24
- pressure_prev: float32 [512, 125], P(('gx', 'gy')), may hold values from -6 to 6
- diag_blocks: float32 [512, 125, 125], P(('gx', 'gy')), as said below
- local_neighbour: int32 [512, 4], P(('gx', 'gy')), may hold values from 0 to 15
- local_blocks: bfloat16 [512, 4, 125, 125], P(('gx', 'gy')), may hold values from -0.5 to 0.5
- send_element: int32 [4, 8, 8, 3], P('gx', 'gy'), may hold values from 0 to 15
- send_count: int32 [4, 8, 8], P('gx', 'gy'), may hold values from 1 to 3
- send_blocks: bfloat16 [4, 8, 8, 3, 125, 125], P('gx', 'gy'), may hold values from -0.5 to 0.5
- receive_element: int32 [4, 8, 8, 3], P('gx', 'gy'), may hold values from 0 to 15
- layer_count: int32 [128], P(('gx', 'gy')), may hold values from 1 to 4
Outputs:
- pressure: float32 [512, 125], P(('gx', 'gy'))
The draws below stay inside these ranges and needn't reach their ends.
Inputs may be any that keep to these rules, and one draw needn't show every extreme that they name: `diag_blocks`: every block is nonsingular.
All inputs are finite; a program needn't handle non-finite values.
Results may differ from the reference program's by a relative error of at most 0.0003.
Values may be sent and summed in bfloat16 or wider, within the bound.
A program may use at most 64 MiB of HBM per device.

```python
import math
import jax
import jax.numpy as jnp
from jax import lax

B = 125
LAYERS = 4
FACES = 4
SLOTS = 3
NS_ITERS = 8
SWEEPS = 3
E_DEV = 16
TOT_COLS = 128
E_TOT = 512
N_GX = 4
N_GY = 8


def draw_diag_blocks(key, part):
    key_scale, key_diagonal, key_spread = jax.random.split(key, 3)
    element_scale = jnp.exp(jax.random.uniform(key_scale, (E_TOT, 1, 1), jnp.float32, 0.0, math.log(4.0)))
    diagonal = jnp.exp(jax.random.uniform(key_diagonal, (E_TOT, B), jnp.float32, math.log(6.0), math.log(48.0)))
    spread_part = jax.random.uniform(key_spread, (E_TOT, B, B), jnp.float32, -0.26, 0.26)
    identity = jnp.eye(B, dtype=jnp.float32)
    matrices = spread_part * (1.0 - identity) + identity * diagonal[:, :, None]
    return (element_scale * matrices).astype(jnp.float32)


def touch_ends(entries, rng, smallest, top_value):
    dims = entries.shape
    spot = [jax.random.randint(jax.random.fold_in(rng, axis), (), 0, dims[axis]) for axis in range(len(dims))]
    entries = entries.at[tuple(spot)].set(smallest)
    longest = dims.index(max(dims))
    spot[longest] = (spot[longest] + 1) % dims[longest]
    return entries.at[tuple(spot)].set(top_value)


def shard_levels(own_key, shape, cuts, low, high):
    gain, own = 1.0, jax.random.fold_in(own_key, 6)
    for position, shards_of in cuts:
        heights = jnp.exp(jax.random.uniform(jax.random.fold_in(own, position), (shards_of,), jnp.float32, low / len(cuts), high / len(cuts)))
        gain = gain * jnp.repeat(heights, shape[position] // shards_of).reshape([-1 if axis == position else 1 for axis in range(len(shape))])
    return gain


def centred(key, extent, deviation, limit, cuts=(), kind=jnp.bfloat16):
    factor_of = shard_levels(key, extent, cuts, -0.22, 0.18) if cuts else 1.0
    drawn = jax.random.normal(key, extent, jnp.float32) * deviation * factor_of
    return jnp.minimum(jnp.maximum(drawn, -limit), limit).astype(kind)


def setup_inputs(seed: int = 0) -> dict:
    keys = jax.random.split(jax.random.key(seed), 11)
    source_term = centred(keys[0], (E_TOT, B), 4.0, 24.0, ((0, 32),), jnp.float32)
    pressure_prev = centred(keys[1], (E_TOT, B), 1.0, 6.0, ((0, 32),), jnp.float32)
    diag_blocks = draw_diag_blocks(jax.random.fold_in(keys[10], 71), 0)
    local_neighbour = touch_ends(jax.random.randint(keys[3], (E_TOT, FACES), 0, E_DEV), jax.random.fold_in(keys[3], 1), 0, E_DEV - 1).astype(jnp.int32)
    local_blocks = centred(keys[4], (E_TOT, FACES, B, B), B ** -0.5, 0.5, ((0, 32),))
    send_element = touch_ends(jax.random.randint(keys[5], (N_GX, N_GY, 8, SLOTS), 0, E_DEV), jax.random.fold_in(keys[5], 1), 0, E_DEV - 1).astype(jnp.int32)
    send_count = touch_ends(jax.random.randint(keys[6], (N_GX, N_GY, 8), 1, SLOTS + 1), jax.random.fold_in(keys[6], 1), 1, SLOTS).astype(jnp.int32)
    send_blocks = centred(keys[7], (N_GX, N_GY, 8, SLOTS, B, B), B ** -0.5, 0.5, ((0, 4), (1, 8)))
    receive_element = touch_ends(jax.random.randint(keys[8], (N_GX, N_GY, 8, SLOTS), 0, E_DEV), jax.random.fold_in(keys[8], 1), 0, E_DEV - 1).astype(jnp.int32)
    layer_count = touch_ends(jax.random.randint(keys[9], (TOT_COLS,), 1, LAYERS + 1), jax.random.fold_in(keys[9], 1), 1, LAYERS).astype(jnp.int32)
    return dict(source_term=source_term, pressure_prev=pressure_prev, diag_blocks=diag_blocks, local_neighbour=local_neighbour, local_blocks=local_blocks, send_element=send_element, send_count=send_count, send_blocks=send_blocks, receive_element=receive_element, layer_count=layer_count)


PRECISE = lax.Precision.HIGHEST
RELAXATION = 0.8
OFFSETS = ((-1, -1), (-1, 0), (-1, 1), (0, -1), (0, 1), (1, -1), (1, 0), (1, 1))


def approx_inverse(blocks):
    magnitude = jnp.abs(blocks)
    column_norm = jnp.max(jnp.sum(magnitude, axis=1), axis=1)
    row_norm = jnp.max(jnp.sum(magnitude, axis=2), axis=1)
    estimate = jnp.swapaxes(blocks, 1, 2) / (column_norm * row_norm)[:, None, None]
    doubled = 2.0 * jnp.eye(blocks.shape[1], dtype=blocks.dtype)
    for iteration in range(NS_ITERS):
        product = jnp.einsum("nij,njk->nik", blocks, estimate, precision=PRECISE)
        estimate = jnp.einsum("nij,njk->nik", estimate, doubled - product, precision=PRECISE)
    return estimate


def pick_rows(source_rows, indices):
    return source_rows[indices]


def face_terms(operand_pair):
    matrices, values = operand_pair
    return jnp.einsum("mfij,mfj->mi", matrices.astype(jnp.float32), values.astype(jnp.float32))


def slot_products(operand_pair):
    matrices, values = operand_pair
    return jnp.einsum("mij,mj->mi", matrices.astype(jnp.float32), values.astype(jnp.float32))


def reference(source_term, pressure_prev, diag_blocks, local_neighbour, local_blocks, send_element, send_count, send_blocks, receive_element, layer_count):
    partitions = N_GX * N_GY
    per_part = E_TOT // partitions
    inverse = lax.map(approx_inverse, diag_blocks.reshape(partitions, per_part, B, B)).reshape(E_TOT, B, B)
    element = jnp.arange(E_TOT, dtype=jnp.int32)
    alive_mask = (element % LAYERS < layer_count[element // LAYERS]).astype(jnp.float32)[:, None]
    pressure = pressure_prev * alive_mask
    slot_open = jnp.arange(SLOTS, dtype=jnp.int32)[None, None, None, :] < send_count[..., None]
    part_start = jnp.arange(partitions, dtype=jnp.int32) * per_part
    targets = (receive_element.reshape(partitions, 8 * SLOTS) + part_start[:, None]).reshape(-1).astype(jnp.int32)
    neighbour_rows = local_neighbour.reshape(partitions, per_part * FACES)
    for sweep_index in range(SWEEPS):
        pressure_half = pressure.astype(jnp.bfloat16)
        by_part = pressure_half.reshape(partitions, per_part, B)
        near_values = jax.vmap(pick_rows)(by_part, neighbour_rows).reshape(partitions, per_part, FACES, B)
        local_term = lax.map(face_terms, (local_blocks.reshape(partitions, per_part, FACES, B, B), near_values)).reshape(E_TOT, B)
        outgoing = jax.vmap(pick_rows)(by_part, send_element.reshape(partitions, 8 * SLOTS)).reshape(N_GX, N_GY, 8, SLOTS, B)
        outgoing = jnp.where(slot_open[..., None], outgoing, jnp.zeros_like(outgoing))
        products = lax.map(slot_products, (send_blocks.reshape(partitions, 8 * SLOTS, B, B), outgoing.reshape(partitions, 8 * SLOTS, B)))
        products = products.reshape(N_GX, N_GY, 8, SLOTS, B)
        padded = jnp.pad(products, ((1, 1), (1, 1), (0, 0), (0, 0), (0, 0)))
        pieces = []
        for direction in range(8):
            step_x, step_y = OFFSETS[direction]
            pieces.append(padded[1 + step_x:1 + step_x + N_GX, 1 + step_y:1 + step_y + N_GY, 7 - direction])
        incoming = jnp.stack(pieces, axis=2)
        remote_term = jax.ops.segment_sum(incoming.reshape(-1, B), targets, num_segments=E_TOT)
        coupled = jnp.einsum("eij,ej->ei", diag_blocks, pressure, precision=PRECISE)
        residual = source_term - (coupled + local_term + remote_term)
        correction = jnp.einsum("eij,ej->ei", inverse, residual, precision=PRECISE)
        pressure = pressure + RELAXATION * alive_mask * correction
    return pressure
```

```python
import functools

import jax
import jax.numpy as jnp
from jax import lax
from jax.experimental import pallas as pl
from jax.experimental.pallas import tpu as pltpu
from jax.sharding import PartitionSpec as P

LAYERS = 4
NS_ITERS = 8
SWEEPS = 3
RELAXATION = 0.8
OFFSETS = ((-1, -1), (-1, 0), (-1, 1), (0, -1), (0, 1), (1, -1), (1, 0), (1, 1))
MESH = pl.DeviceIdType.MESH
BF16 = jnp.bfloat16
F32 = jnp.float32
W = 128
GROUP = 16
CHUNK = 4


def dot(a, b):
    return jnp.dot(a, b, preferred_element_type=F32)


def split(x):
    hi = x.astype(BF16)
    return hi, (x - hi.astype(F32)).astype(BF16)


def padded(x, rows):
    return jnp.pad(x, ((0, rows - x.shape[0]), (0, W - x.shape[1])))


def kernel(
    source_ref,
    prev_ref,
    diag_hbm,
    near_ref,
    local_hbm,
    send_el_ref,
    count_ref,
    send_hbm,
    recv_el_ref,
    layer_ref,
    out_ref,
    diag_in,
    local_in,
    send_in,
    fx_f,
    fx_s,
    blocks,
    sends,
    sendbuf,
    recvbuf,
    load_sem,
    send_sem,
    recv_sem,
):
    elements, width = source_ref.shape
    faces = near_ref.shape[1]
    slots = send_el_ref.shape[3]
    nx, ny = lax.axis_size("gx"), lax.axis_size("gy")
    gx, gy = lax.axis_index("gx"), lax.axis_index("gy")

    def there(k):
        a, b = OFFSETS[k]
        x, y = gx + a, gy + b
        return (x >= 0) & (x < nx) & (y >= 0) & (y < ny), (x, y)

    load_send = pltpu.make_async_copy(send_hbm.at[0, 0], send_in, load_sem.at[0])
    load_diag = pltpu.make_async_copy(diag_hbm, diag_in, load_sem.at[1])
    load_local = pltpu.make_async_copy(local_hbm, local_in, load_sem.at[2])
    load_send.start()
    load_diag.start()
    load_local.start()

    barrier = pltpu.get_barrier_semaphore()
    present = jnp.int32(0)
    for k in range(8):
        exists, target = there(k)
        present = present + exists.astype(jnp.int32)

        @pl.when(exists)
        def _():
            pl.semaphore_signal(barrier, inc=1, device_id=target, device_id_type=MESH)

        @pl.when(jnp.logical_not(exists))
        def _():
            for t in range(SWEEPS):
                recvbuf[t, k] = jnp.zeros((8, W), F32)

    lane = lax.broadcasted_iota(jnp.int32, (W, W), 1)
    lane_row = lax.broadcasted_iota(jnp.int32, (1, W), 1)
    element = lane % GROUP
    group = lane // GROUP

    index = jnp.full((1, W), -1, jnp.int32)
    for f in range(faces):
        for e in range(elements):
            index = jnp.where(lane_row == f * GROUP + e, near_ref[e, f], index)
    for k in range(8):
        count = count_ref[0, 0, k]
        for s in range(slots):
            chosen = jnp.where(s < count, send_el_ref[0, 0, k, s], -1)
            index = jnp.where(lane_row == 64 + 8 * k + s, chosen, index)
    select = (lax.broadcasted_iota(jnp.int32, (W, W), 0) == index).astype(F32).astype(BF16)
    row8 = lax.broadcasted_iota(jnp.int32, (8, W), 0)
    scatter_rows = []
    for k in range(8):
        target_el = jnp.full((8, W), -1, jnp.int32)
        for s in range(slots):
            target_el = jnp.where(row8 == s, recv_el_ref[0, 0, k, s], target_el)
        scatter_rows.append(target_el)
    scatter = jnp.concatenate(scatter_rows, axis=0)
    scatter = (scatter == lax.broadcasted_iota(jnp.int32, (64, W), 1) % GROUP).astype(F32).astype(BF16)

    depth = jnp.zeros((1, W), jnp.int32)
    for c in range(elements // LAYERS):
        depth = jnp.where((lane_row % GROUP) // LAYERS == c, layer_ref[c], depth)
    alive = (lane_row % LAYERS < depth).astype(F32)

    def nodes_first(x):
        rows = padded(x, elements)
        return jnp.concatenate([rows] * (W // GROUP), axis=0).T

    source = nodes_first(source_ref[...])
    pressure = nodes_first(prev_ref[...]) * alive

    def gathered(p):
        return dot(p.astype(BF16), select)

    def send_part(t, g):
        zero = jnp.zeros_like(g)
        low = jnp.where((lane >= 64) & (lane < 96), g, zero)
        high = jnp.where(lane >= 96, g, zero)
        rhs = jnp.concatenate([low, high], axis=0).astype(BF16)
        acc = zero
        for k in range(4):
            res = dot(sends[k].reshape(slots * W, 2 * W), rhs)
            for s in range(slots):
                acc = jnp.where((lane >= 64) & (lane % 32 == 8 * k + s), res[s * W : (s + 1) * W], acc)
        sendbuf[t] = acc.T[64:].reshape(8, 8, W)
        for k in range(8):
            exists, target = there(k)

            @pl.when(exists)
            def _():
                remote(t, k, 7 - k, target).start()

    def remote(t, k, landing, target):
        return pltpu.make_async_remote_copy(
            src_ref=sendbuf.at[t, k],
            dst_ref=recvbuf.at[t, landing],
            send_sem=send_sem.at[t, k],
            recv_sem=recv_sem.at[t, landing],
            device_id=target,
            device_id_type=MESH,
        )

    load_send.wait()

    for k in range(4):

        def prepare_send(s, carry, k=k):
            for half in range(2):
                sends[k, s, :, half * W : (half + 1) * W] = padded(send_in[k + 4 * half, s], W)
            return carry

        lax.fori_loop(0, slots, prepare_send, 0)
    pl.semaphore_wait(barrier, present)
    g = gathered(pressure)
    send_part(0, g)

    load_diag.wait()

    def doubled(x):
        return jnp.concatenate([x, x], axis=0)

    def store_split(e, start, x):
        hi, lo = split(x)
        rows = x.shape[0]
        fx_s[e, start : start + rows, 0:W] = hi
        fx_s[e, start : start + rows, W : 2 * W] = lo

    def prepare_diag(i, carry):
        for u in range(CHUNK):
            e = i * CHUNK + u
            m = padded(diag_in[e], W)
            magnitude = jnp.abs(m)
            column_norm = jnp.max(jnp.sum(magnitude, axis=0, keepdims=True), axis=1, keepdims=True)
            row_norm = jnp.max(jnp.sum(magnitude, axis=1, keepdims=True), axis=0, keepdims=True)
            x = m.T * (1.0 / (column_norm * row_norm))
            hi, lo = split(m)
            blocks[e, :, 4 * W : 5 * W] = hi
            blocks[e, :, 5 * W : 6 * W] = lo
            fx_f[e, W:] = x
            store_split(e, W, x)
            res = dot(blocks[e, :, 4 * W :], doubled(fx_s[e, W:]))
            f = res[:, :W] + res[:, W:]
            fx_f[e, :W] = f
            store_split(e, 0, f)
        return carry

    lax.fori_loop(0, elements // CHUNK, prepare_diag, 0)

    def step(k, carry):
        for e in range(elements):
            both = fx_s[e]
            res = dot(both, doubled(both[:W]))
            new = 2.0 * fx_f[e] - (res[:, :W] + res[:, W:])
            fx_f[e] = new
            store_split(e, 0, new)
        return carry

    lax.fori_loop(0, NS_ITERS - 1, step, 0)
    for e in range(elements):
        res = dot(fx_s[e, W:], doubled(fx_s[e, :W]))
        store_split(e, W, 2.0 * fx_f[e, W:] - (res[:, :W] + res[:, W:]))

    load_local.wait()

    def prepare_local(e, carry):
        for f in range(faces):
            blocks[e, :, f * W : (f + 1) * W] = padded(local_in[e, f], W)
        return carry

    lax.fori_loop(0, elements, prepare_local, 0)

    def per_element(load, rhs):
        acc = jnp.zeros((W, W), F32)
        for i in range(elements // CHUNK):
            res = dot(load(i * CHUNK), rhs)
            for u in range(CHUNK):
                acc = jnp.where(element == i * CHUNK + u, res[u * W : (u + 1) * W], acc)
        return acc

    for t in range(SWEEPS):
        zero = jnp.zeros_like(g)
        hi, lo = split(pressure)
        near = [jnp.where(group == f, g, zero).astype(BF16) for f in range(faces)]
        own = jnp.where(group == 4, hi.astype(F32), jnp.where(group == 5, lo.astype(F32), zero)).astype(BF16)
        acc = per_element(
            lambda e: blocks[e : e + CHUNK].reshape(CHUNK * W, 6 * W),
            jnp.concatenate(near + [own, own], axis=0),
        )
        for shift in (64, 32, 16):
            acc = acc + pltpu.roll(acc, shift, 1)
        local = source - acc

        for k in range(8):
            exists, target = there(k)

            @pl.when(exists)
            def _():
                remote(t, k, k, target).wait_recv()

        arrived = recvbuf[t].reshape(64, W).T
        arrived_hi, arrived_lo = split(arrived)
        residual = local - (dot(arrived_hi, scatter) + dot(arrived_lo, scatter))
        hi, lo = split(residual)
        rhs = jnp.where(group % 2 == 0, hi.astype(F32), lo.astype(F32)).astype(BF16)
        acc = per_element(
            lambda e: fx_s[e : e + CHUNK, W:].reshape(CHUNK * W, 2 * W), doubled(rhs)
        )
        acc = acc + pltpu.roll(acc, 16, 1)
        pressure = pressure + RELAXATION * alive * acc
        if t + 1 < SWEEPS:
            g = gathered(pressure)
            send_part(t + 1, g)

    out_ref[...] = pressure.T[:elements, :width]

    for t in range(SWEEPS):
        for k in range(8):
            exists, target = there(k)

            @pl.when(exists)
            def _():
                remote(t, k, k, target).wait_send()


def on_device(*args):
    source, prev, diag, near, local, send_el, count, send, recv_el, layers = args
    elements, width = source.shape
    faces = near.shape[1]
    slots = send_el.shape[3]
    vmem = pl.BlockSpec(memory_space=pltpu.VMEM)
    smem = pl.BlockSpec(memory_space=pltpu.SMEM)
    hbm = pl.BlockSpec(memory_space=pl.ANY)
    return pl.pallas_call(
        kernel,
        out_shape=jax.ShapeDtypeStruct(source.shape, F32),
        in_specs=[vmem, vmem, hbm, smem, hbm, smem, smem, hbm, smem, smem],
        out_specs=vmem,
        scratch_shapes=[
            pltpu.VMEM(diag.shape, F32),
            pltpu.VMEM(local.shape, BF16),
            pltpu.VMEM(send.shape[2:], BF16),
            pltpu.VMEM((elements, 2 * W, W), F32),
            pltpu.VMEM((elements, 2 * W, 2 * W), BF16),
            pltpu.VMEM((elements, W, 6 * W), BF16),
            pltpu.VMEM((4, slots, W, 2 * W), BF16),
            pltpu.VMEM((SWEEPS, 8, 8, W), F32),
            pltpu.VMEM((SWEEPS, 8, 8, W), F32),
            pltpu.SemaphoreType.DMA((3,)),
            pltpu.SemaphoreType.DMA((SWEEPS, 8)),
            pltpu.SemaphoreType.DMA((SWEEPS, 8)),
        ],
        compiler_params=pltpu.CompilerParams(
            collective_id=0, has_side_effects=True, vmem_limit_bytes=48 * 1024 * 1024
        ),
    )(*args)


def solution(mesh):
    return jax.shard_map(
        on_device,
        mesh=mesh,
        in_specs=(
            P(("gx", "gy"), None),
            P(("gx", "gy"), None),
            P(("gx", "gy"), None, None),
            P(("gx", "gy"), None),
            P(("gx", "gy"), None, None, None),
            P("gx", "gy", None, None),
            P("gx", "gy", None),
            P("gx", "gy", None, None, None, None),
            P("gx", "gy", None, None),
            P(("gx", "gy")),
        ),
        out_specs=P(("gx", "gy"), None),
        check_vma=False,
    )
```

```python
import functools

import jax
import jax.numpy as jnp
from jax import lax
from jax.experimental import pallas as pl
from jax.experimental.pallas import tpu as pltpu
from jax.sharding import PartitionSpec as P

LAYERS = 4
NS_ITERS = 8
SWEEPS = 3
RELAXATION = 0.8
OFFSETS = ((-1, -1), (-1, 0), (-1, 1), (0, -1), (0, 1), (1, -1), (1, 0), (1, 1))
MESH = pl.DeviceIdType.MESH
BF16 = jnp.bfloat16
F32 = jnp.float32
W = 128
GROUP = 16
CHUNK = 4


def dot(a, b):
    return jnp.dot(a, b, preferred_element_type=F32)


def split(x):
    hi = x.astype(BF16)
    return hi, (x - hi.astype(F32)).astype(BF16)


def padded(x, rows):
    return jnp.pad(x, ((0, rows - x.shape[0]), (0, W - x.shape[1])))


def kernel(
    source_ref,
    prev_ref,
    diag_in,
    near_ref,
    local_in,
    send_el_ref,
    count_ref,
    send_in,
    recv_el_ref,
    layer_ref,
    out_ref,
    send_wide,
    fx_f,
    fx_s,
    blocks,
    sends,
    sendbuf,
    recvbuf,
    send_sem,
    recv_sem,
):
    elements, width = source_ref.shape
    faces = near_ref.shape[0]
    slots = send_el_ref.shape[0]
    nx, ny = lax.axis_size("gx"), lax.axis_size("gy")
    gx, gy = lax.axis_index("gx"), lax.axis_index("gy")

    def there(k):
        a, b = OFFSETS[k]
        x, y = gx + a, gy + b
        return (x >= 0) & (x < nx) & (y >= 0) & (y < ny), (x, y)

    barrier = pltpu.get_barrier_semaphore()
    present = jnp.int32(0)
    for k in range(8):
        exists, target = there(k)
        present = present + exists.astype(jnp.int32)

        @pl.when(exists)
        def _():
            pl.semaphore_signal(barrier, inc=1, device_id=target, device_id_type=MESH)

        @pl.when(jnp.logical_not(exists))
        def _():
            for t in range(SWEEPS):
                recvbuf[t, k] = jnp.zeros((8, W), F32)

    lane = lax.broadcasted_iota(jnp.int32, (W, W), 1)
    lane_row = lax.broadcasted_iota(jnp.int32, (1, W), 1)
    element = lane % GROUP
    group = lane // GROUP

    index = jnp.full((1, W), -1, jnp.int32)
    for f in range(faces):
        for e in range(elements):
            index = jnp.where(lane_row == f * GROUP + e, near_ref[f, e], index)
    for k in range(8):
        count = count_ref[0, 0, k]
        for s in range(slots):
            chosen = jnp.where(s < count, send_el_ref[s, 0, k], -1)
            index = jnp.where(lane_row == 64 + 8 * k + s, chosen, index)
    select = (lax.broadcasted_iota(jnp.int32, (W, W), 0) == index).astype(F32).astype(BF16)
    row8 = lax.broadcasted_iota(jnp.int32, (8, W), 0)
    scatter_rows = []
    for k in range(8):
        target_el = jnp.full((8, W), -1, jnp.int32)
        for s in range(slots):
            target_el = jnp.where(row8 == s, recv_el_ref[s, 0, k], target_el)
        scatter_rows.append(target_el)
    scatter = jnp.concatenate(scatter_rows, axis=0)
    scatter = (scatter == lax.broadcasted_iota(jnp.int32, (64, W), 1) % GROUP).astype(F32).astype(BF16)

    depth = jnp.zeros((1, W), jnp.int32)
    for c in range(elements // LAYERS):
        depth = jnp.where((lane_row % GROUP) // LAYERS == c, layer_ref[c], depth)
    alive = (lane_row % LAYERS < depth).astype(F32)

    def nodes_first(x):
        rows = padded(x, elements)
        return jnp.concatenate([rows] * (W // GROUP), axis=0).T

    source = nodes_first(source_ref[...])
    pressure = nodes_first(prev_ref[...]) * alive

    def gathered(p):
        return dot(p.astype(BF16), select)

    def send_part(t, g):
        zero = jnp.zeros_like(g)
        low = jnp.where((lane >= 64) & (lane < 96), g, zero)
        high = jnp.where(lane >= 96, g, zero)
        rhs = jnp.concatenate([low, high], axis=0).astype(BF16)
        acc = zero
        for k in range(4):
            res = dot(sends[k].reshape(slots * W, 2 * W), rhs)
            for s in range(slots):
                acc = jnp.where((lane >= 64) & (lane % 32 == 8 * k + s), res[s * W : (s + 1) * W], acc)
        sendbuf[t] = acc.T[64:].reshape(8, 8, W)
        for k in range(8):
            exists, target = there(k)

            @pl.when(exists)
            def _():
                remote(t, k, 7 - k, target).start()

    def remote(t, k, landing, target):
        return pltpu.make_async_remote_copy(
            src_ref=sendbuf.at[t, k],
            dst_ref=recvbuf.at[t, landing],
            send_sem=send_sem.at[t, k],
            recv_sem=recv_sem.at[t, landing],
            device_id=target,
            device_id_type=MESH,
        )

    send_wide[...] = send_in[...].astype(F32)
    for k in range(4):
        for s in range(slots):
            for half in range(2):
                rows = pl.ds(s * width * 8 + k + 4 * half, width, stride=8)
                block = padded(send_wide[rows, :], W).astype(BF16)
                sends[k, s, :, half * W : (half + 1) * W] = block
    pl.semaphore_wait(barrier, present)
    g = gathered(pressure)
    send_part(0, g)

    def doubled(x):
        return jnp.concatenate([x, x], axis=0)

    def store_split(e, start, x):
        hi, lo = split(x)
        rows = x.shape[0]
        fx_s[e, start : start + rows, 0:W] = hi
        fx_s[e, start : start + rows, W : 2 * W] = lo

    def prepare_diag(i, carry):
        for u in range(CHUNK):
            e = i * CHUNK + u
            m = padded(diag_in[pl.ds(e, width, stride=elements), :], W)
            magnitude = jnp.abs(m)
            column_norm = jnp.max(jnp.sum(magnitude, axis=0, keepdims=True), axis=1, keepdims=True)
            row_norm = jnp.max(jnp.sum(magnitude, axis=1, keepdims=True), axis=0, keepdims=True)
            x = m.T * (1.0 / (column_norm * row_norm))
            hi, lo = split(m)
            blocks[e, :, 4 * W : 5 * W] = hi
            blocks[e, :, 5 * W : 6 * W] = lo
            fx_f[e, W:] = x
            store_split(e, W, x)
            res = dot(blocks[e, :, 4 * W :], doubled(fx_s[e, W:]))
            f = res[:, :W] + res[:, W:]
            fx_f[e, :W] = f
            store_split(e, 0, f)
        return carry

    lax.fori_loop(0, elements // CHUNK, prepare_diag, 0)

    def step(k, carry):
        for e in range(elements):
            both = fx_s[e]
            res = dot(both, doubled(both[:W]))
            new = 2.0 * fx_f[e] - (res[:, :W] + res[:, W:])
            fx_f[e] = new
            store_split(e, 0, new)
        return carry

    lax.fori_loop(0, NS_ITERS - 1, step, 0)
    for e in range(elements):
        res = dot(fx_s[e, W:], doubled(fx_s[e, :W]))
        store_split(e, W, 2.0 * fx_f[e, W:] - (res[:, :W] + res[:, W:]))

    def prepare_local(e, carry):
        for f in range(faces):
            blocks[e, :, f * W : (f + 1) * W] = padded(local_in[e, f], W)
        return carry

    lax.fori_loop(0, elements, prepare_local, 0)

    def per_element(load, rhs):
        acc = jnp.zeros((W, W), F32)
        for i in range(elements // CHUNK):
            res = dot(load(i * CHUNK), rhs)
            for u in range(CHUNK):
                acc = jnp.where(element == i * CHUNK + u, res[u * W : (u + 1) * W], acc)
        return acc

    for t in range(SWEEPS):
        zero = jnp.zeros_like(g)
        hi, lo = split(pressure)
        near = [jnp.where(group == f, g, zero).astype(BF16) for f in range(faces)]
        own = jnp.where(group == 4, hi.astype(F32), jnp.where(group == 5, lo.astype(F32), zero)).astype(BF16)
        acc = per_element(
            lambda e: blocks[e : e + CHUNK].reshape(CHUNK * W, 6 * W),
            jnp.concatenate(near + [own, own], axis=0),
        )
        for shift in (64, 32, 16):
            acc = acc + pltpu.roll(acc, shift, 1)
        local = source - acc

        for k in range(8):
            exists, target = there(k)

            @pl.when(exists)
            def _():
                remote(t, k, k, target).wait_recv()

        arrived = recvbuf[t].reshape(64, W).T
        arrived_hi, arrived_lo = split(arrived)
        residual = local - (dot(arrived_hi, scatter) + dot(arrived_lo, scatter))
        hi, lo = split(residual)
        rhs = jnp.where(group % 2 == 0, hi.astype(F32), lo.astype(F32)).astype(BF16)
        acc = per_element(
            lambda e: fx_s[e : e + CHUNK, W:].reshape(CHUNK * W, 2 * W), doubled(rhs)
        )
        acc = acc + pltpu.roll(acc, 16, 1)
        pressure = pressure + RELAXATION * alive * acc
        if t + 1 < SWEEPS:
            g = gathered(pressure)
            send_part(t + 1, g)

    out_ref[...] = pressure.T[:elements, :width]

    for t in range(SWEEPS):
        for k in range(8):
            exists, target = there(k)

            @pl.when(exists)
            def _():
                remote(t, k, k, target).wait_send()


def on_device(*args):
    source, prev, diag, near, local, send_el, count, send, recv_el, layers = args
    elements, width = source.shape
    faces = near.shape[1]
    slots = send_el.shape[3]
    diag = diag.transpose(1, 0, 2).reshape(width * elements, width)
    send = send[0, 0].transpose(1, 2, 0, 3).reshape(slots * width * 8, width)
    near = near.T
    send_el = send_el.transpose(3, 0, 1, 2).reshape(slots, 1, 8)
    recv_el = recv_el.transpose(3, 0, 1, 2).reshape(slots, 1, 8)
    vmem = pl.BlockSpec(memory_space=pltpu.VMEM)
    smem = pl.BlockSpec(memory_space=pltpu.SMEM)
    return pl.pallas_call(
        kernel,
        out_shape=jax.ShapeDtypeStruct(source.shape, F32),
        in_specs=[vmem, vmem, vmem, smem, vmem, smem, smem, vmem, smem, smem],
        out_specs=vmem,
        scratch_shapes=[
            pltpu.VMEM(send.shape, F32),
            pltpu.VMEM((elements, 2 * W, W), F32),
            pltpu.VMEM((elements, 2 * W, 2 * W), BF16),
            pltpu.VMEM((elements, W, 6 * W), BF16),
            pltpu.VMEM((4, slots, W, 2 * W), BF16),
            pltpu.VMEM((SWEEPS, 8, 8, W), F32),
            pltpu.VMEM((SWEEPS, 8, 8, W), F32),
            pltpu.SemaphoreType.DMA((SWEEPS, 8)),
            pltpu.SemaphoreType.DMA((SWEEPS, 8)),
        ],
        compiler_params=pltpu.CompilerParams(
            collective_id=0, has_side_effects=True, vmem_limit_bytes=48 * 1024 * 1024
        ),
    )(source, prev, diag, near, local, send_el, count, send, recv_el, layers)


def solution(mesh):
    return jax.shard_map(
        on_device,
        mesh=mesh,
        in_specs=(
            P(("gx", "gy"), None),
            P(("gx", "gy"), None),
            P(("gx", "gy"), None, None),
            P(("gx", "gy"), None),
            P(("gx", "gy"), None, None, None),
            P("gx", "gy", None, None),
            P("gx", "gy", None),
            P("gx", "gy", None, None, None, None),
            P("gx", "gy", None, None),
            P(("gx", "gy")),
        ),
        out_specs=P(("gx", "gy"), None),
        check_vma=False,
    )
```

```python
import functools

import jax
import jax.numpy as jnp
from jax import lax
from jax.experimental import pallas as pl
from jax.experimental.pallas import tpu as pltpu
from jax.sharding import PartitionSpec as P

LAYERS = 4
NS_ITERS = 8
SWEEPS = 3
RELAXATION = 0.8
OFFSETS = ((-1, -1), (-1, 0), (-1, 1), (0, -1), (0, 1), (1, -1), (1, 0), (1, 1))
FAR_FIRST = (0, 2, 5, 7, 1, 6, 3, 4)
ROWS = 4
MESH = pl.DeviceIdType.MESH
BF16 = jnp.bfloat16
F32 = jnp.float32
W = 128
GROUP = 16
CHUNK = 4


def dot(a, b):
    return jnp.dot(a, b, preferred_element_type=F32)


def split(x):
    hi = x.astype(BF16)
    return hi, (x - hi.astype(F32)).astype(BF16)


def padded(x, rows):
    return jnp.pad(x, ((0, rows - x.shape[0]), (0, W - x.shape[1])))


def kernel(
    source_ref,
    prev_ref,
    diag_in,
    near_ref,
    local_in,
    send_el_ref,
    count_ref,
    send_in,
    recv_el_ref,
    layer_ref,
    out_ref,
    send_wide,
    local_wide,
    fx_f,
    fx_s,
    blocks,
    sends,
    sendbuf,
    recvbuf,
    send_sem,
    recv_sem,
):
    elements, width = source_ref.shape
    faces = near_ref.shape[0]
    slots = send_el_ref.shape[0]
    nx, ny = lax.axis_size("gx"), lax.axis_size("gy")
    gx, gy = lax.axis_index("gx"), lax.axis_index("gy")

    def there(k):
        a, b = OFFSETS[k]
        x, y = gx + a, gy + b
        return (x >= 0) & (x < nx) & (y >= 0) & (y < ny), (x, y)

    barrier = pltpu.get_barrier_semaphore()
    present = jnp.int32(0)
    for k in range(8):
        exists, target = there(k)
        present = present + exists.astype(jnp.int32)

        @pl.when(exists)
        def _():
            pl.semaphore_signal(barrier, inc=1, device_id=target, device_id_type=MESH)

        @pl.when(jnp.logical_not(exists))
        def _():
            for t in range(SWEEPS):
                recvbuf[t, k] = jnp.zeros((ROWS, W), F32)

    lane = lax.broadcasted_iota(jnp.int32, (W, W), 1)
    lane_row = lax.broadcasted_iota(jnp.int32, (1, W), 1)
    element = lane % GROUP
    group = lane // GROUP

    index = jnp.full((1, W), -1, jnp.int32)
    for f in range(faces):
        for e in range(elements):
            index = jnp.where(lane_row == f * GROUP + e, near_ref[f, e], index)
    for k in range(8):
        count = count_ref[0, 0, k]
        for s in range(slots):
            chosen = jnp.where(s < count, send_el_ref[s, 0, k], -1)
            index = jnp.where(lane_row == 64 + ROWS * k + s, chosen, index)
    select = (lax.broadcasted_iota(jnp.int32, (W, W), 0) == index).astype(F32).astype(BF16)
    row = lax.broadcasted_iota(jnp.int32, (8 * ROWS, W), 0)
    scatter = jnp.full((8 * ROWS, W), -1, jnp.int32)
    for k in range(8):
        for s in range(slots):
            scatter = jnp.where(row == ROWS * k + s, recv_el_ref[s, 0, k], scatter)
    scatter = (scatter == lax.broadcasted_iota(jnp.int32, (8 * ROWS, W), 1) % GROUP).astype(F32).astype(BF16)

    depth = jnp.zeros((1, W), jnp.int32)
    for c in range(elements // LAYERS):
        depth = jnp.where((lane_row % GROUP) // LAYERS == c, layer_ref[c], depth)
    alive = (lane_row % LAYERS < depth).astype(F32)

    def nodes_first(x):
        rows = padded(x, elements)
        return jnp.concatenate([rows] * (W // GROUP), axis=0).T

    source = nodes_first(source_ref[...])
    pressure = nodes_first(prev_ref[...]) * alive

    def gathered(p):
        return dot(p.astype(BF16), select)

    def send_part(t, g):
        zero = jnp.zeros_like(g)
        low = jnp.where((lane >= 64) & (lane < 64 + 4 * ROWS), g, zero)
        high = jnp.where(lane >= 64 + 4 * ROWS, g, zero)
        rhs = jnp.concatenate([low, high], axis=0).astype(BF16)
        acc = zero
        for k in range(4):
            res = dot(sends[k].reshape(slots * W, 2 * W), rhs)
            for s in range(slots):
                acc = jnp.where((lane >= 64) & (lane < 64 + 8 * ROWS) & (lane % (4 * ROWS) == ROWS * k + s), res[s * W : (s + 1) * W], acc)
        outgoing = acc.T
        for k in range(8):
            sendbuf[t, k] = outgoing[64 + ROWS * k : 64 + ROWS * (k + 1)]
        for k in FAR_FIRST:
            exists, target = there(k)

            @pl.when(exists)
            def _():
                remote(t, k, 7 - k, target).start()

    def remote(t, k, landing, target):
        return pltpu.make_async_remote_copy(
            src_ref=sendbuf.at[t, k],
            dst_ref=recvbuf.at[t, landing],
            send_sem=send_sem.at[t, k],
            recv_sem=recv_sem.at[t, landing],
            device_id=target,
            device_id_type=MESH,
        )

    def doubled(x):
        return jnp.concatenate([x, x], axis=0)

    def store_split(e, start, x):
        hi, lo = split(x)
        rows = x.shape[0]
        fx_s[e, start : start + rows, 0:W] = hi
        fx_s[e, start : start + rows, W : 2 * W] = lo

    def prepare_diag(i, carry):
        for u in range(2 * CHUNK):
            e = i * 2 * CHUNK + u
            m = padded(diag_in[pl.ds(e, width, stride=elements), :], W)
            magnitude = jnp.abs(m)
            column_norm = jnp.max(jnp.sum(magnitude, axis=0, keepdims=True), axis=1, keepdims=True)
            row_norm = jnp.max(jnp.sum(magnitude, axis=1, keepdims=True), axis=0, keepdims=True)
            x = m.T * (1.0 / (column_norm * row_norm))
            hi, lo = split(m)
            blocks[e, :, 4 * W : 5 * W] = hi
            blocks[e, :, 5 * W : 6 * W] = lo
            fx_f[e, W:] = x
            store_split(e, W, x)
            res = dot(blocks[e, :, 4 * W :], doubled(fx_s[e, W:]))
            f = res[:, :W] + res[:, W:]
            fx_f[e, :W] = f
            store_split(e, 0, f)
        return carry

    lax.fori_loop(0, elements // (2 * CHUNK), prepare_diag, 0)

    def step(k, carry):
        for e in range(elements):
            both = fx_s[e]
            res = dot(both, doubled(both[:W]))
            new = 2.0 * fx_f[e] - (res[:, :W] + res[:, W:])
            fx_f[e] = new
            store_split(e, 0, new)
        return carry

    def prepare_local(k, carry):
        rows = CHUNK * width * faces
        local_wide[...] = local_in[pl.ds(pl.multiple_of(k * rows, 16), rows), :].astype(F32)
        for u in range(CHUNK):
            for f in range(faces):
                block = local_wide[pl.ds(u * width * faces + f, width, stride=faces), :]
                blocks[k * CHUNK + u, :, f * W : (f + 1) * W] = padded(block, W).astype(BF16)
        return step(k, carry)

    send_wide[...] = send_in[...].astype(F32)
    for k in range(4):
        for s in range(slots):
            for half in range(2):
                rows = pl.ds(s * width * 8 + k + 4 * half, width, stride=8)
                block = padded(send_wide[rows, :], W).astype(BF16)
                sends[k, s, :, half * W : (half + 1) * W] = block
    step(0, 0)
    pl.semaphore_wait(barrier, present)
    g = gathered(pressure)
    send_part(0, g)

    chunks = elements // CHUNK
    lax.fori_loop(0, chunks, prepare_local, 0)
    lax.fori_loop(chunks, NS_ITERS - 2, step, 0)
    for e in range(elements):
        res = dot(fx_s[e, W:], doubled(fx_s[e, :W]))
        store_split(e, W, 2.0 * fx_f[e, W:] - (res[:, :W] + res[:, W:]))

    def per_element(load, rhs):
        acc = jnp.zeros((W, W), F32)
        for i in range(elements // CHUNK):
            res = dot(load(i * CHUNK), rhs)
            for u in range(CHUNK):
                acc = jnp.where(element == i * CHUNK + u, res[u * W : (u + 1) * W], acc)
        return acc

    for t in range(SWEEPS):
        zero = jnp.zeros_like(g)
        hi, lo = split(pressure)
        near = [jnp.where(group == f, g, zero).astype(BF16) for f in range(faces)]
        own = jnp.where(group == 4, hi.astype(F32), jnp.where(group == 5, lo.astype(F32), zero)).astype(BF16)
        acc = per_element(
            lambda e: blocks[e : e + CHUNK].reshape(CHUNK * W, 6 * W),
            jnp.concatenate(near + [own, own], axis=0),
        )
        for shift in (64, 32, 16):
            acc = acc + pltpu.roll(acc, shift, 1)
        local = source - acc

        for k in range(8):
            exists, target = there(k)

            @pl.when(exists)
            def _():
                remote(t, k, k, target).wait_recv()

        arrived = jnp.concatenate([recvbuf[t, k] for k in range(8)], axis=0).T
        arrived_hi, arrived_lo = split(arrived)
        residual = local - (dot(arrived_hi, scatter) + dot(arrived_lo, scatter))
        hi, lo = split(residual)
        rhs = jnp.where(group % 2 == 0, hi.astype(F32), lo.astype(F32)).astype(BF16)
        acc = per_element(
            lambda e: fx_s[e : e + CHUNK, W:].reshape(CHUNK * W, 2 * W), doubled(rhs)
        )
        acc = acc + pltpu.roll(acc, 16, 1)
        pressure = pressure + RELAXATION * alive * acc
        if t + 1 < SWEEPS:
            g = gathered(pressure)
            send_part(t + 1, g)

    out_ref[...] = pressure.T[:elements, :width]

    for t in range(SWEEPS):
        for k in range(8):
            exists, target = there(k)

            @pl.when(exists)
            def _():
                remote(t, k, k, target).wait_send()


def on_device(*args):
    source, prev, diag, near, local, send_el, count, send, recv_el, layers = args
    elements, width = source.shape
    faces = near.shape[1]
    slots = send_el.shape[3]
    diag = diag.transpose(1, 0, 2).reshape(width * elements, width)
    send = send[0, 0].transpose(1, 2, 0, 3).reshape(slots * width * 8, width)
    local = local.transpose(0, 2, 1, 3).reshape(elements * width * faces, width)
    near = near.T
    send_el = send_el.transpose(3, 0, 1, 2).reshape(slots, 1, 8)
    recv_el = recv_el.transpose(3, 0, 1, 2).reshape(slots, 1, 8)
    vmem = pl.BlockSpec(memory_space=pltpu.VMEM)
    smem = pl.BlockSpec(memory_space=pltpu.SMEM)
    return pl.pallas_call(
        kernel,
        out_shape=jax.ShapeDtypeStruct(source.shape, F32),
        in_specs=[vmem, vmem, vmem, smem, vmem, smem, smem, vmem, smem, smem],
        out_specs=vmem,
        scratch_shapes=[
            pltpu.VMEM(send.shape, F32),
            pltpu.VMEM((CHUNK * width * faces, width), F32),
            pltpu.VMEM((elements, 2 * W, W), F32),
            pltpu.VMEM((elements, 2 * W, 2 * W), BF16),
            pltpu.VMEM((elements, W, 6 * W), BF16),
            pltpu.VMEM((4, slots, W, 2 * W), BF16),
            pltpu.VMEM((SWEEPS, 8, ROWS, W), F32),
            pltpu.VMEM((SWEEPS, 8, ROWS, W), F32),
            pltpu.SemaphoreType.DMA((SWEEPS, 8)),
            pltpu.SemaphoreType.DMA((SWEEPS, 8)),
        ],
        compiler_params=pltpu.CompilerParams(
            collective_id=0, has_side_effects=True, vmem_limit_bytes=48 * 1024 * 1024
        ),
    )(source, prev, diag, near, local, send_el, count, send, recv_el, layers)


def solution(mesh):
    return jax.shard_map(
        on_device,
        mesh=mesh,
        in_specs=(
            P(("gx", "gy"), None),
            P(("gx", "gy"), None),
            P(("gx", "gy"), None, None),
            P(("gx", "gy"), None),
            P(("gx", "gy"), None, None, None),
            P("gx", "gy", None, None),
            P("gx", "gy", None),
            P("gx", "gy", None, None, None, None),
            P("gx", "gy", None, None),
            P(("gx", "gy")),
        ),
        out_specs=P(("gx", "gy"), None),
        check_vma=False,
    )
```

```python
import functools

import jax
import jax.numpy as jnp
from jax import lax
from jax.experimental import pallas as pl
from jax.experimental.pallas import tpu as pltpu
from jax.sharding import PartitionSpec as P

LAYERS = 4
NS_ITERS = 8
SWEEPS = 3
RELAXATION = 0.8
OFFSETS = ((-1, -1), (-1, 0), (-1, 1), (0, -1), (0, 1), (1, -1), (1, 0), (1, 1))
FAR_FIRST = (0, 2, 5, 7, 1, 6, 3, 4)
ROWS = 4
MESH = pl.DeviceIdType.MESH
BF16 = jnp.bfloat16
F32 = jnp.float32
W = 128
GROUP = 16
CHUNK = 4


def dot(a, b):
    return jnp.dot(a, b, preferred_element_type=F32)


def split(x):
    hi = x.astype(BF16)
    return hi, (x - hi.astype(F32)).astype(BF16)


def padded(x, rows):
    return jnp.pad(x, ((0, rows - x.shape[0]), (0, W - x.shape[1])))


def kernel(
    source_ref,
    prev_ref,
    diag_in,
    near_ref,
    local_in,
    send_el_ref,
    count_ref,
    send_in,
    recv_el_ref,
    layer_ref,
    out_ref,
    send_wide,
    fx_f,
    fx_s,
    blocks,
    sends,
    sendbuf,
    recvbuf,
    send_sem,
    recv_sem,
):
    elements, width = source_ref.shape
    faces = near_ref.shape[0]
    slots = send_el_ref.shape[0]
    nx, ny = lax.axis_size("gx"), lax.axis_size("gy")
    gx, gy = lax.axis_index("gx"), lax.axis_index("gy")

    def there(k):
        a, b = OFFSETS[k]
        x, y = gx + a, gy + b
        return (x >= 0) & (x < nx) & (y >= 0) & (y < ny), (x, y)

    barrier = pltpu.get_barrier_semaphore()
    present = jnp.int32(0)
    for k in range(8):
        exists, target = there(k)
        present = present + exists.astype(jnp.int32)

        @pl.when(exists)
        def _():
            pl.semaphore_signal(barrier, inc=1, device_id=target, device_id_type=MESH)

        @pl.when(jnp.logical_not(exists))
        def _():
            for t in range(SWEEPS):
                recvbuf[t, k] = jnp.zeros((ROWS, W), F32)

    lane = lax.broadcasted_iota(jnp.int32, (W, W), 1)
    lane_row = lax.broadcasted_iota(jnp.int32, (1, W), 1)
    element = lane % GROUP
    group = lane // GROUP

    index = jnp.full((1, W), -1, jnp.int32)
    for f in range(faces):
        for e in range(elements):
            index = jnp.where(lane_row == f * GROUP + e, near_ref[f, e], index)
    for k in range(8):
        count = count_ref[0, 0, k]
        for s in range(slots):
            chosen = jnp.where(s < count, send_el_ref[s, 0, k], -1)
            index = jnp.where(lane_row == 64 + ROWS * k + s, chosen, index)
    select = (lax.broadcasted_iota(jnp.int32, (W, W), 0) == index).astype(F32).astype(BF16)
    row = lax.broadcasted_iota(jnp.int32, (8 * ROWS, W), 0)
    scatter = jnp.full((8 * ROWS, W), -1, jnp.int32)
    for k in range(8):
        for s in range(slots):
            scatter = jnp.where(row == ROWS * k + s, recv_el_ref[s, 0, k], scatter)
    scatter = (scatter == lax.broadcasted_iota(jnp.int32, (8 * ROWS, W), 1) % GROUP).astype(F32).astype(BF16)

    depth = jnp.zeros((1, W), jnp.int32)
    for c in range(elements // LAYERS):
        depth = jnp.where((lane_row % GROUP) // LAYERS == c, layer_ref[c], depth)
    alive = (lane_row % LAYERS < depth).astype(F32)

    def nodes_first(x):
        rows = padded(x, elements)
        return jnp.concatenate([rows] * (W // GROUP), axis=0).T

    source = nodes_first(source_ref[...])
    pressure = nodes_first(prev_ref[...]) * alive

    def gathered(p):
        return dot(p.astype(BF16), select)

    def send_part(t, g):
        zero = jnp.zeros_like(g)
        low = jnp.where((lane >= 64) & (lane < 64 + 4 * ROWS), g, zero)
        high = jnp.where(lane >= 64 + 4 * ROWS, g, zero)
        rhs = jnp.concatenate([low, high], axis=0).astype(BF16)
        acc = zero
        for k in range(4):
            res = dot(sends[k].reshape(slots * W, 2 * W), rhs)
            for s in range(slots):
                acc = jnp.where((lane >= 64) & (lane < 64 + 8 * ROWS) & (lane % (4 * ROWS) == ROWS * k + s), res[s * W : (s + 1) * W], acc)
        outgoing = acc.T
        for k in range(8):
            sendbuf[t, k] = outgoing[64 + ROWS * k : 64 + ROWS * (k + 1)]
        for k in FAR_FIRST:
            exists, target = there(k)

            @pl.when(exists)
            def _():
                remote(t, k, 7 - k, target).start()

    def remote(t, k, landing, target):
        return pltpu.make_async_remote_copy(
            src_ref=sendbuf.at[t, k],
            dst_ref=recvbuf.at[t, landing],
            send_sem=send_sem.at[t, k],
            recv_sem=recv_sem.at[t, landing],
            device_id=target,
            device_id_type=MESH,
        )

    def doubled(x):
        return jnp.concatenate([x, x], axis=0)

    def store_split(e, start, x):
        hi, lo = split(x)
        rows = x.shape[0]
        fx_s[e, start : start + rows, 0:W] = hi
        fx_s[e, start : start + rows, W : 2 * W] = lo

    def prepare_diag(i, carry):
        for u in range(2 * CHUNK):
            e = i * 2 * CHUNK + u
            m = padded(diag_in[pl.ds(e, width, stride=elements), :], W)
            magnitude = jnp.abs(m)
            column_norm = jnp.max(jnp.sum(magnitude, axis=0, keepdims=True), axis=1, keepdims=True)
            row_norm = jnp.max(jnp.sum(magnitude, axis=1, keepdims=True), axis=0, keepdims=True)
            x = m.T * (1.0 / (column_norm * row_norm))
            hi, lo = split(m)
            blocks[e, :, 4 * W : 5 * W] = hi
            blocks[e, :, 5 * W : 6 * W] = lo
            fx_f[e, W:] = x
            store_split(e, W, x)
            res = dot(blocks[e, :, 4 * W :], doubled(fx_s[e, W:]))
            f = res[:, :W] + res[:, W:]
            fx_f[e, :W] = f
            store_split(e, 0, f)
        return carry

    lax.fori_loop(0, elements // (2 * CHUNK), prepare_diag, 0)

    def step(k, carry):
        for e in range(elements):
            both = fx_s[e]
            res = dot(both, doubled(both[:W]))
            new = 2.0 * fx_f[e] - (res[:, :W] + res[:, W:])
            fx_f[e] = new
            store_split(e, 0, new)
        return carry

    def prepare_local(e, carry):
        for f in range(faces):
            blocks[e, :, f * W : (f + 1) * W] = padded(local_in[e, f], W)
        return carry

    send_wide[...] = send_in[...].astype(F32)
    for k in range(4):
        for s in range(slots):
            for half in range(2):
                rows = pl.ds(s * width * 8 + k + 4 * half, width, stride=8)
                block = padded(send_wide[rows, :], W).astype(BF16)
                sends[k, s, :, half * W : (half + 1) * W] = block
    step(0, 0)
    pl.semaphore_wait(barrier, present)
    g = gathered(pressure)
    send_part(0, g)

    lax.fori_loop(0, elements, prepare_local, 0)
    lax.fori_loop(1, NS_ITERS - 1, step, 0)
    for e in range(elements):
        res = dot(fx_s[e, W:], doubled(fx_s[e, :W]))
        store_split(e, W, 2.0 * fx_f[e, W:] - (res[:, :W] + res[:, W:]))

    def per_element(load, rhs):
        acc = jnp.zeros((W, W), F32)
        for i in range(elements // CHUNK):
            res = dot(load(i * CHUNK), rhs)
            for u in range(CHUNK):
                acc = jnp.where(element == i * CHUNK + u, res[u * W : (u + 1) * W], acc)
        return acc

    for t in range(SWEEPS):
        zero = jnp.zeros_like(g)
        hi, lo = split(pressure)
        near = [jnp.where(group == f, g, zero).astype(BF16) for f in range(faces)]
        own = jnp.where(group == 4, hi.astype(F32), jnp.where(group == 5, lo.astype(F32), zero)).astype(BF16)
        acc = per_element(
            lambda e: blocks[e : e + CHUNK].reshape(CHUNK * W, 6 * W),
            jnp.concatenate(near + [own, own], axis=0),
        )
        for shift in (64, 32, 16):
            acc = acc + pltpu.roll(acc, shift, 1)
        local = source - acc

        for k in range(8):
            exists, target = there(k)

            @pl.when(exists)
            def _():
                remote(t, k, k, target).wait_recv()

        arrived = jnp.concatenate([recvbuf[t, k] for k in range(8)], axis=0).T
        arrived_hi, arrived_lo = split(arrived)
        residual = local - (dot(arrived_hi, scatter) + dot(arrived_lo, scatter))
        hi, lo = split(residual)
        rhs = jnp.where(group % 2 == 0, hi.astype(F32), lo.astype(F32)).astype(BF16)
        acc = per_element(
            lambda e: fx_s[e : e + CHUNK, W:].reshape(CHUNK * W, 2 * W), doubled(rhs)
        )
        acc = acc + pltpu.roll(acc, 16, 1)
        pressure = pressure + RELAXATION * alive * acc
        if t + 1 < SWEEPS:
            g = gathered(pressure)
            send_part(t + 1, g)

    out_ref[...] = pressure.T[:elements, :width]

    for t in range(SWEEPS):
        for k in range(8):
            exists, target = there(k)

            @pl.when(exists)
            def _():
                remote(t, k, k, target).wait_send()


def on_device(*args):
    source, prev, diag, near, local, send_el, count, send, recv_el, layers = args
    elements, width = source.shape
    faces = near.shape[1]
    slots = send_el.shape[3]
    diag = diag.transpose(1, 0, 2).reshape(width * elements, width)
    send = send[0, 0].transpose(1, 2, 0, 3).reshape(slots * width * 8, width)
    near = near.T
    send_el = send_el.transpose(3, 0, 1, 2).reshape(slots, 1, 8)
    recv_el = recv_el.transpose(3, 0, 1, 2).reshape(slots, 1, 8)
    vmem = pl.BlockSpec(memory_space=pltpu.VMEM)
    smem = pl.BlockSpec(memory_space=pltpu.SMEM)
    return pl.pallas_call(
        kernel,
        out_shape=jax.ShapeDtypeStruct(source.shape, F32),
        in_specs=[vmem, vmem, vmem, smem, vmem, smem, smem, vmem, smem, smem],
        out_specs=vmem,
        scratch_shapes=[
            pltpu.VMEM(send.shape, F32),
            pltpu.VMEM((elements, 2 * W, W), F32),
            pltpu.VMEM((elements, 2 * W, 2 * W), BF16),
            pltpu.VMEM((elements, W, 6 * W), BF16),
            pltpu.VMEM((4, slots, W, 2 * W), BF16),
            pltpu.VMEM((SWEEPS, 8, ROWS, W), F32),
            pltpu.VMEM((SWEEPS, 8, ROWS, W), F32),
            pltpu.SemaphoreType.DMA((SWEEPS, 8)),
            pltpu.SemaphoreType.DMA((SWEEPS, 8)),
        ],
        compiler_params=pltpu.CompilerParams(
            collective_id=0, has_side_effects=True, vmem_limit_bytes=48 * 1024 * 1024
        ),
    )(source, prev, diag, near, local, send_el, count, send, recv_el, layers)


def solution(mesh):
    return jax.shard_map(
        on_device,
        mesh=mesh,
        in_specs=(
            P(("gx", "gy"), None),
            P(("gx", "gy"), None),
            P(("gx", "gy"), None, None),
            P(("gx", "gy"), None),
            P(("gx", "gy"), None, None, None),
            P("gx", "gy", None, None),
            P("gx", "gy", None),
            P("gx", "gy", None, None, None, None),
            P("gx", "gy", None, None),
            P(("gx", "gy")),
        ),
        out_specs=P(("gx", "gy"), None),
        check_vma=False,
    )
```
